1024 devices in a mesh: row: 8 (over x), col: 16 (over z, core), layer: 8 (over y).
Axes of the slice: x: 8, y: 8, z: 8, core: 2. Of those that a mesh axis runs over, the one named last changes fastest.
Arguments:
- three_centre: bfloat16 [2048, 48, 2048], P('layer', 'row', 'col'), may hold values from -6 to 6
- occ_density: bfloat16 [2048, 2048], P('col', ('row', 'layer')), may hold values from -1 to 1, as said below
- virt_density: bfloat16 [2048, 2048], P('layer', ('row', 'col')), may hold values from -1 to 1, as said below
- pair_mask: int32 [16, 16], replicated, may hold values 0 or 1
- occ_mask: int32 [16, 16], replicated, may hold values from 0 to 1, as said below
- virt_mask: int32 [16, 16], replicated, may hold values from 0 to 1, as said below
- block_sizes: int32 [16], replicated, may hold values from 64 to 128
Outputs:
- transformed: bfloat16 [2048, 48, 2048], P('layer', 'row', 'col')
The draws below stay inside these ranges and needn't reach their ends.
Inputs may be any that keep to these rules, and one draw needn't show every extreme that they name: `occ_density`: symmetric. `virt_density`: symmetric. `occ_mask`: symmetric, ones on the diagonal. `virt_mask`: symmetric, ones on the diagonal.
All inputs are finite; a program needn't handle non-finite values.
Results may differ from the reference program's by a relative error of at most 0.0049.
Values may be sent and summed in bfloat16 or wider, within the bound.
A program may use at most 32 MiB of HBM per device.

```python
import math
import jax
import jax.numpy as jnp
from jax import lax

BLOCK = 128
NB = 16
NAO = 2048
NAUX = 48


def symmetric_density(key):
    entries = jax.random.normal(key, (NAO, NAO), jnp.float32)
    return ((entries + entries.T) * (1.4 / math.sqrt(2.0 * NAO))).astype(jnp.bfloat16)


def symmetric_mask(key):
    raw_bits = jax.random.randint(key, (NB, NB), 0, 2, jnp.int32)
    diagonal = (jnp.arange(NB)[:, None] == jnp.arange(NB)[None, :]).astype(jnp.int32)
    return jnp.maximum(jnp.maximum(raw_bits, raw_bits.T), diagonal)


def draw_occ_density(key, part):
    key = jax.random.fold_in(key, 11)
    return symmetric_density(key)


def draw_virt_density(key, part):
    key = jax.random.fold_in(key, 12)
    return symmetric_density(key)


def draw_occ_mask(key, part):
    key = jax.random.fold_in(key, 21)
    return symmetric_mask(key)


def draw_virt_mask(key, part):
    key = jax.random.fold_in(key, 22)
    return symmetric_mask(key)


def plant(values, rng, smallest, high):
    spot = [jax.random.randint(jax.random.fold_in(rng, axis), (), 0, length) for axis, length in enumerate(values.shape)]
    main_axis = values.shape.index(max(values.shape))
    beside = spot[:main_axis] + [(spot[main_axis] + 1) % values.shape[main_axis]] + spot[main_axis + 1:]
    return values.at[tuple(spot)].set(smallest).at[tuple(beside)].set(high)


def shard_levels(stream_key, dims, shards, smallest, high):
    gain = 1.0
    for position, shards_of in shards:
        heights = jax.random.uniform(jax.random.fold_in(jax.random.fold_in(stream_key, 6), position), (shards_of,), jnp.float32, smallest / len(shards), high / len(shards))
        gain = gain * jnp.repeat(jnp.exp(heights), dims[position] // shards_of).reshape((-1,) + (1,) * (len(dims) - 1 - position))
    return gain


def gaussian(own_key, shape, width, most, shards=(), kind=jnp.bfloat16):
    gain = shard_levels(own_key, shape, shards, -0.22, 0.18) if shards else 1.0
    values = jax.random.normal(own_key, shape, jnp.float32) * width * gain
    return jnp.minimum(jnp.maximum(values, -most), most).astype(kind)


def setup_inputs(seed: int = 0) -> dict:
    seeds = jax.random.split(jax.random.key(seed), 8)
    return {
        "three_centre": gaussian(seeds[0], (NAO, NAUX, NAO), 1.0, 6.0, ((0, 8), (1, 8), (2, 16))),
        "occ_density": draw_occ_density(jax.random.fold_in(seeds[7], 71), 0),
        "virt_density": draw_virt_density(jax.random.fold_in(seeds[7], 71), 0),
        "pair_mask": plant((jax.random.randint(seeds[3], (NB, NB), 0, 4) < 3).astype(jnp.int32), jax.random.fold_in(seeds[3], 1), 0, 1),
        "occ_mask": draw_occ_mask(jax.random.fold_in(seeds[7], 71), 0),
        "virt_mask": draw_virt_mask(jax.random.fold_in(seeds[7], 71), 0),
        "block_sizes": plant(jax.random.randint(seeds[6], (NB,), BLOCK // 2, BLOCK + 1), jax.random.fold_in(seeds[6], 1), BLOCK // 2, BLOCK).astype(jnp.int32),
    }


def reference(three_centre, occ_density, virt_density, pair_mask, occ_mask, virt_mask, block_sizes):
    slots = jnp.arange(NAO, dtype=jnp.int32)
    block_of = (slots // BLOCK).astype(jnp.int32)
    living = ((slots % BLOCK) < block_sizes[block_of]).astype(jnp.float32)

    def masked(density, mask_table):
        keep_mask = mask_table[block_of][:, block_of].astype(jnp.float32) * living[:, None] * living[None, :]
        return (density.astype(jnp.float32) * keep_mask).astype(jnp.bfloat16)

    occ = masked(occ_density, occ_mask)
    virt = masked(virt_density, virt_mask)
    pair_keep = pair_mask[block_of][:, block_of] > 0
    pair_data = jnp.where(pair_keep[:, None, :], three_centre, jnp.zeros((), jnp.bfloat16))

    def one_aux(aux_slab):
        occ_half = jnp.dot(aux_slab, occ, preferred_element_type=jnp.float32).astype(jnp.bfloat16)
        return jnp.dot(virt, occ_half, preferred_element_type=jnp.float32).astype(jnp.bfloat16)

    result = lax.map(one_aux, jnp.moveaxis(pair_data, 1, 0))
    return jnp.moveaxis(result, 0, 1)
```

```python
import jax
import jax.numpy as jnp
from jax import lax
from jax.experimental import pallas as pl
from jax.experimental.pallas import tpu as pltpu
from jax.sharding import PartitionSpec as P

MESH = pl.DeviceIdType.MESH
BLOCK = 128
N = 8
RELATIVE = (0, -1, 1, -2, 2, -3, 3, 4)
PLACE = {0: 0, -1: 1, 1: 2, -2: 3, 2: 4, -3: 5, 3: 6, 4: 7, -4: 7}
STAGES = (((0, 1),), ((1, 2),), ((2, 3), (2, 4)))
EDGES = tuple(edge for stage in STAGES for edge in stage)


def kernel(
    x_hbm, occ_hbm, virt_hbm, pair_mask, occ_mask, virt_mask, sizes,
    out_hbm,
    x_raw, occ_raw, virt_raw, xa, xb, ha, gb, og, vs, vg, outs,
    load_sem, store_sem, first_send, first_recv, dens_send, dens_recv,
    ring_send, ring_recv, sib_send, sib_recv, vsib_send, vsib_recv,
):
    x, col, y = lax.axis_index("row"), lax.axis_index("col"), lax.axis_index("layer")
    z, core = col // 2, lax.rem(col, 2)

    def wrap(i):
        return lax.rem(i + 2 * N, N)

    def device(axis, step):
        if axis == "x":
            return (wrap(x + step), col, y)
        if axis == "y":
            return (x, col, wrap(y + step))
        return (x, wrap(z + step) * 2 + core, y)

    sibling = (x, z * 2 + 1 - core, y)

    barrier = pltpu.get_barrier_semaphore()
    partners = [sibling]
    partners += [device("y", s) for s in range(1, N)] + [device("z", s) for s in range(1, N)]
    partners += [device("x", s) for s in (1, -1, 2, -2)]
    for partner in partners:
        pl.semaphore_signal(barrier, inc=1, device_id=partner, device_id_type=MESH)
    loads = [
        pltpu.make_async_copy(occ_hbm, occ_raw, load_sem.at[6]),
        pltpu.make_async_copy(virt_hbm, virt_raw, load_sem.at[7]),
    ] + [pltpu.make_async_copy(x_hbm.at[p], x_raw.at[p], load_sem.at[p]) for p in range(6)]
    for load in loads:
        load.start()

    loads[0].wait()
    n_block = 2 * x + y // 4
    n_living = (lax.rem(y, 4) * 32 + lax.broadcasted_iota(jnp.int32, (32, 128), 0)) < sizes[n_block]
    k_living = lax.broadcasted_iota(jnp.int32, (32, 128), 1) < sizes[col]
    o_keep = n_living & k_living & (occ_mask[n_block, col] > 0)
    og[x, y] = jnp.where(o_keep, occ_raw[...].astype(jnp.float32), 0.0).astype(jnp.bfloat16)
    loads[1].wait()
    m_block = 2 * x + col // 8
    m_living = (lax.rem(col, 8) * 16 + lax.broadcasted_iota(jnp.int32, (16, 128), 0)) < sizes[m_block]
    lane = lax.broadcasted_iota(jnp.int32, (16, 128), 1)
    for half in range(2):
        a_block = 2 * y + half
        v_keep = m_living & (lane < sizes[a_block]) & (virt_mask[a_block, m_block] > 0)
        part = virt_raw[:, half * 128 : half * 128 + 128].astype(jnp.float32)
        vs[z, :, half * 128 : half * 128 + 128] = jnp.where(v_keep, part, 0.0).astype(jnp.bfloat16)
    keep = [jnp.where(pair_mask[2 * y + half, col] > 0, 1.0, 0.0).astype(jnp.bfloat16) for half in range(2)]
    for p in range(6):
        loads[2 + p].wait()
        if p < 3:
            for half in range(2):
                rows = pl.ds(half * 128, 128)
                xa[p, 0, core, rows] = x_raw[p, rows] * keep[half]
        else:
            for half in range(2):
                part = x_raw[p, pl.ds(half * 128, 128)] * keep[half]
                xb[p - 3, 0, pl.ds(half * 4, 4)] = part.reshape(4, 2, 16, 128)

    pl.semaphore_wait(barrier, len(partners))

    started = []

    def start(copy):
        copy.start()
        started.append(copy)
        return copy

    def remote(src, dst, send, recv, to):
        return start(pltpu.make_async_remote_copy(
            src_ref=src, dst_ref=dst, send_sem=send, recv_sem=recv, device_id=to, device_id_type=MESH))

    def window(buf, p, place, half):
        if buf is xa or buf is gb:
            ref = buf.at[p, place, core]
            return ref if half is None else ref.at[pl.ds(half * 128, 128)]
        ref = buf.at[p, place]
        return ref if half is None else ref.at[pl.ds(half * 4, 4)]

    class Gather:
        def __init__(self, index, axis, buf, p):
            self.index, self.axis, self.buf, self.p = index, axis, buf, p
            self.copies = {}

        def send(self, way, edge):
            step = 1 - 2 * way
            at, to = EDGES[edge]
            half = way if to == 4 else None
            self.copies[way, edge] = remote(
                window(self.buf, self.p, PLACE[-step * at], half),
                window(self.buf, self.p, PLACE[-step * to], half),
                ring_send.at[self.index, way, edge],
                ring_recv.at[self.index, way, edge],
                device(self.axis, step * (to - at)),
            )

        def arrived(self, way, edge):
            self.copies[way, edge].wait_recv()

    class Density:
        def __init__(self, index):
            self.index, self.copies = index, {}

        def send(self, way, edge):
            step = 1 - 2 * way
            at, to = EDGES[edge]
            group = wrap(x - step * at)
            ref = og.at[group] if self.index == 0 else vg.at[group, core]
            if to == 4:
                ref = ref.at[pl.ds(way * (4 if self.index == 0 else 128), 4 if self.index == 0 else 128)]
            self.copies[way, edge] = remote(
                ref, ref, dens_send.at[self.index, way, edge], dens_recv.at[self.index, way, edge],
                device("x", step * (to - at)))

        def arrived(self, way, edge):
            self.copies[way, edge].wait_recv()

    def share(buf, p, index, stage):
        first, count = ((0, 1), (1, 2), (3, 2), (5, 3))[stage]
        ref = buf.at[p, pl.ds(first, count), core]
        return remote(ref, ref, sib_send.at[index, stage], sib_recv.at[index, stage], sibling)

    def share_virt(i, group):
        ref = vg.at[group, core]
        return remote(ref, ref, vsib_send.at[i], vsib_recv.at[i], sibling)

    first = []
    for s in (4, 3, -3, 2, -2, 1, -1):
        slot = s % N
        first.append(remote(og.at[x, y], og.at[x, y], first_send.at[0, slot], first_recv.at[0, slot], device("y", s)))
        first.append(remote(vs.at[z], vs.at[z], first_send.at[1, slot], first_recv.at[1, slot], device("z", s)))

    phase1 = []
    for p in range(3):
        phase1 += [Gather(2 * p, "z", xa, p), Gather(2 * p + 1, "y", xb, p)]
    shares = {}

    for g in phase1:
        for way in range(2):
            g.send(way, 0)
    for g in phase1:
        if g.buf is xa:
            shares[g.index, 0] = share(xa, g.p, g.index, 0)

    for g in phase1:
        for way in range(2):
            g.arrived(way, 0)
            g.send(way, 1)
        if g.buf is xa:
            shares[g.index, 1] = share(xa, g.p, g.index, 1)

    for copy in first:
        copy.wait_recv()
    vg[x, core] = vs[...].reshape(128, 256).T
    dens = [Density(0), Density(1)]
    for way in range(2):
        for d in dens:
            d.send(way, 0)
    vshares = [share_virt(0, x)]

    for g in phase1:
        for way in range(2):
            g.arrived(way, 1)
            g.send(way, 2)
            g.send(way, 3)
        if g.buf is xa:
            shares[g.index, 2] = share(xa, g.p, g.index, 2)

    for way in range(2):
        for d in dens:
            d.arrived(way, 0)
            d.send(way, 1)
        vshares.append(share_virt(1 + way, wrap(x - (1 - 2 * way))))
    for way in range(2):
        for d in dens:
            d.arrived(way, 1)
            d.send(way, 2)
            d.send(way, 3)
        vshares.append(share_virt(3 + way, wrap(x - 2 * (1 - 2 * way))))

    for g in phase1:
        for way in range(2):
            g.arrived(way, 2)
        for way in range(2):
            g.arrived(way, 3)
        if g.buf is xa:
            shares[g.index, 3] = share(xa, g.p, g.index, 3)

    for way in range(2):
        for d in dens:
            d.arrived(way, 2)
        vshares.append(share_virt(5 + way, wrap(x - 3 * (1 - 2 * way))))
    for way in range(2):
        for d in dens:
            d.arrived(way, 3)
    vshares.append(share_virt(7, wrap(x + 4)))

    def times_occ(buf, p):
        total = jnp.zeros((256, 128), jnp.float32)
        for place in range(N):
            group = wrap(z + RELATIVE[place])
            left = jnp.concatenate([buf[p, place, 0], buf[p, place, 1]], axis=1)
            total += jnp.dot(left, og[group].reshape(256, 128), preferred_element_type=jnp.float32)
        return total.astype(jnp.bfloat16)

    def virt_times(buf, p):
        total = jnp.zeros((256, 128), jnp.float32)
        for place in range(N):
            group = wrap(y + RELATIVE[place])
            left = jnp.concatenate([vg[group, 0], vg[group, 1]], axis=1)
            right = jnp.concatenate(
                [buf[p, place, :, 0].reshape(128, 128), buf[p, place, :, 1].reshape(128, 128)], axis=0)
            total += jnp.dot(left, right, preferred_element_type=jnp.float32)
        return total.astype(jnp.bfloat16)

    phase2 = []
    for p in range(3):
        phase2 += [Gather(6 + 2 * p, "y", ha, p), Gather(7 + 2 * p, "z", gb, p)]
    for g in phase2:
        if g.buf is ha:
            for stage in range(4):
                shares[2 * g.p, stage].wait_recv()
            ha[g.p, 0] = times_occ(xa, g.p).reshape(8, 2, 16, 128)
        else:
            if g.p == 0:
                for copy in vshares:
                    copy.wait_recv()
            gb[g.p, 0, core] = virt_times(xb, g.p)
        for way in range(2):
            g.send(way, 0)
        if g.buf is gb:
            shares[g.index, 0] = share(gb, g.p, g.index - 1, 0)
    for g in phase2:
        for way in range(2):
            g.arrived(way, 0)
            g.send(way, 1)
        if g.buf is gb:
            shares[g.index, 1] = share(gb, g.p, g.index - 1, 1)
    for g in phase2:
        for way in range(2):
            g.arrived(way, 1)
            g.send(way, 2)
            g.send(way, 3)
        if g.buf is gb:
            shares[g.index, 2] = share(gb, g.p, g.index - 1, 2)
    stores = []
    for g in phase2:
        for way in range(2):
            g.arrived(way, 2)
        for way in range(2):
            g.arrived(way, 3)
        if g.buf is gb:
            shares[g.index, 3] = share(gb, g.p, g.index - 1, 3)
        else:
            outs[g.p] = virt_times(ha, g.p)
            store = pltpu.make_async_copy(outs.at[g.p], out_hbm.at[g.p], store_sem.at[g.p])
            store.start()
            stores.append(store)
    for g in phase2:
        if g.buf is gb:
            for stage in range(4):
                shares[g.index, stage].wait_recv()
            outs[3 + g.p] = times_occ(gb, g.p)
            store = pltpu.make_async_copy(outs.at[3 + g.p], out_hbm.at[3 + g.p], store_sem.at[3 + g.p])
            store.start()
            stores.append(store)
    for copy in started:
        copy.wait_send()
    for store in stores:
        store.wait()


def on_device(three_centre, occ_density, virt_density, pair_mask, occ_mask, virt_mask, block_sizes):
    bf16 = jnp.bfloat16
    any_space = pl.BlockSpec(memory_space=pl.ANY)
    scalars = pl.BlockSpec(memory_space=pltpu.SMEM)
    dma = pltpu.SemaphoreType.DMA
    edges = len(EDGES)
    out = pl.pallas_call(
        kernel,
        out_shape=jax.ShapeDtypeStruct((6, 256, 128), bf16),
        in_specs=[any_space] * 3 + [scalars] * 4,
        out_specs=any_space,
        scratch_shapes=[
            pltpu.VMEM((6, 256, 128), bf16),
            pltpu.VMEM((32, 128), bf16),
            pltpu.VMEM((16, 256), bf16),
            pltpu.VMEM((3, N, 2, 256, 128), bf16),
            pltpu.VMEM((3, N, 8, 2, 16, 128), bf16),
            pltpu.VMEM((3, N, 8, 2, 16, 128), bf16),
            pltpu.VMEM((3, N, 2, 256, 128), bf16),
            pltpu.VMEM((N, 8, 32, 128), bf16),
            pltpu.VMEM((N, 16, 256), bf16),
            pltpu.VMEM((N, 2, 256, 128), bf16),
            pltpu.VMEM((6, 256, 128), bf16),
            dma((8,)),
            dma((6,)),
            dma((2, N)),
            dma((2, N)),
            dma((2, 2, edges)),
            dma((2, 2, edges)),
            dma((12, 2, edges)),
            dma((12, 2, edges)),
            dma((12, 4)),
            dma((12, 4)),
            dma((N,)),
            dma((N,)),
        ],
        compiler_params=pltpu.CompilerParams(
            collective_id=0, has_side_effects=True, vmem_limit_bytes=32 << 20
        ),
        cost_estimate=pl.CostEstimate(flops=1610612736, bytes_accessed=1 << 20, transcendentals=0),
        name="transform",
    )(
        jnp.transpose(three_centre, (1, 0, 2)), occ_density.T, virt_density.T,
        pair_mask, occ_mask, virt_mask, block_sizes,
    )
    return jnp.transpose(out, (1, 0, 2))


def solution(mesh):
    placed = (
        P("layer", "row", "col"),
        P("col", ("row", "layer")),
        P("layer", ("row", "col")),
        P(),
        P(),
        P(),
        P(),
    )
    return jax.shard_map(
        on_device, mesh=mesh, in_specs=placed, out_specs=P("layer", "row", "col"), check_vma=False
    )
```

```python
import jax
import jax.numpy as jnp
from jax import lax
from jax.experimental import pallas as pl
from jax.experimental.pallas import tpu as pltpu
from jax.sharding import PartitionSpec as P

MESH = pl.DeviceIdType.MESH
BLOCK = 128
N = 8
RELATIVE = (0, -1, 1, -2, 2, -3, 3, 4)
PLACE = {0: 0, -1: 1, 1: 2, -2: 3, 2: 4, -3: 5, 3: 6, 4: 7, -4: 7}
STAGES = (((0, 1),), ((1, 2),), ((2, 3), (2, 4)))
EDGES = tuple(edge for stage in STAGES for edge in stage)
STAGE_OF = ((0,), (1,), (2, 3))


def kernel(
    x_hbm, occ_hbm, virt_hbm, pair_hbm, occ_mask_hbm, virt_mask_hbm, sizes_hbm,
    out_hbm,
    pair_mask, occ_mask, virt_mask, sizes,
    x_raw, occ_raw, virt_raw, xa, xb, ha, gb, og, og_other, vs, vg, mine, give, got, outs,
    load_sem, store_sem, first_send, first_recv, dens_send, dens_recv,
    ring_send, ring_recv, part_send, part_recv, sib_send, sib_recv,
):
    x, col, y = lax.axis_index("row"), lax.axis_index("col"), lax.axis_index("layer")
    z, core = col // 2, lax.rem(col, 2)

    def wrap(i):
        return lax.rem(i + 2 * N, N)

    def device(axis, step):
        if axis == "x":
            return (wrap(x + step), col, y)
        if axis == "y":
            return (x, col, wrap(y + step))
        return (x, wrap(z + step) * 2 + core, y)

    sibling = (x, z * 2 + 1 - core, y)

    barrier = pltpu.get_barrier_semaphore()
    partners = [sibling]
    partners += [device("y", s) for s in range(1, N)] + [device("z", s) for s in range(1, N)]
    partners += [device("x", s) for s in (1, -1, 2, -2)]
    for partner in partners:
        pl.semaphore_signal(barrier, inc=1, device_id=partner, device_id_type=MESH)
    pairs = (
        (sizes_hbm, sizes), (occ_mask_hbm, occ_mask), (virt_mask_hbm, virt_mask), (pair_hbm, pair_mask),
        (occ_hbm, occ_raw), (virt_hbm, virt_raw),
    ) + tuple((x_hbm.at[p], x_raw.at[p]) for p in range(6))
    loads = [pltpu.make_async_copy(src, dst, load_sem.at[i]) for i, (src, dst) in enumerate(pairs)]
    for load in loads:
        load.start()

    for load in loads[:5]:
        load.wait()
    n_block = 2 * x + y // 4
    n_living = (lax.rem(y, 4) * 32 + lax.broadcasted_iota(jnp.int32, (32, 128), 0)) < sizes[n_block]
    k_living = lax.broadcasted_iota(jnp.int32, (32, 128), 1) < sizes[col]
    o_keep = n_living & k_living & (occ_mask[n_block, col] > 0)
    og[x, y] = jnp.where(o_keep, occ_raw[...].astype(jnp.float32), 0.0).astype(jnp.bfloat16)
    loads[5].wait()
    m_block = 2 * x + col // 8
    m_living = (lax.rem(col, 8) * 16 + lax.broadcasted_iota(jnp.int32, (16, 128), 0)) < sizes[m_block]
    lane = lax.broadcasted_iota(jnp.int32, (16, 128), 1)
    for half in range(2):
        a_block = 2 * y + half
        v_keep = m_living & (lane < sizes[a_block]) & (virt_mask[a_block, m_block] > 0)
        part = virt_raw[:, half * 128 : half * 128 + 128].astype(jnp.float32)
        vs[z, :, half * 128 : half * 128 + 128] = jnp.where(v_keep, part, 0.0).astype(jnp.bfloat16)
    keep = [jnp.where(pair_mask[2 * y + half, col] > 0, 1.0, 0.0).astype(jnp.bfloat16) for half in range(2)]
    for p in range(6):
        loads[6 + p].wait()
        if p < 3:
            for half in range(2):
                rows = pl.ds(half * 128, 128)
                xa[p, 0, rows] = x_raw[p, rows] * keep[half]
        else:
            for half in range(2):
                part = x_raw[p, pl.ds(half * 128, 128)] * keep[half]
                xb[p - 3, 0, pl.ds(half * 4, 4)] = part.reshape(4, 2, 16, 128)

    pl.semaphore_wait(barrier, len(partners))

    started = []

    class Flight:
        def __init__(self, copy):
            self.copy, self.waited = copy, False
            copy.start()
            started.append(self)

        def wait_recv(self):
            if not self.waited:
                self.copy.wait_recv()
            self.waited = True

    def remote(src, dst, send, recv, to):
        return Flight(pltpu.make_async_remote_copy(
            src_ref=src, dst_ref=dst, send_sem=send, recv_sem=recv, device_id=to, device_id_type=MESH))

    def window(buf, p, place, half):
        ref = buf.at[p, place]
        if half is None:
            return ref
        return ref.at[pl.ds(half * 128, 128)] if buf is xa or buf is gb else ref.at[pl.ds(half * 4, 4)]

    class Gather:
        def __init__(self, index, axis, buf, p):
            self.index, self.axis, self.buf, self.p = index, axis, buf, p
            self.copies = {}

        def send(self, way, edge):
            step = 1 - 2 * way
            at, to = EDGES[edge]
            half = way if to == 4 else None
            self.copies[way, edge] = remote(
                window(self.buf, self.p, PLACE[-step * at], half),
                window(self.buf, self.p, PLACE[-step * to], half),
                ring_send.at[self.index, way, edge],
                ring_recv.at[self.index, way, edge],
                device(self.axis, step * (to - at)),
            )

        def advance(self, stage):
            for way in range(2):
                if stage > 0:
                    self.copies[way, STAGE_OF[stage - 1][0]].wait_recv()
                for edge in STAGE_OF[stage]:
                    self.send(way, edge)

        def finish(self):
            for copy in self.copies.values():
                copy.wait_recv()

    class Density(Gather):
        def __init__(self, index):
            self.index, self.copies = index, {}

        def send(self, way, edge):
            step = 1 - 2 * way
            at, to = EDGES[edge]
            group = wrap(x - step * at)
            ref = og.at[group] if self.index == 0 else vg.at[group, core]
            if to == 4:
                half = 4 if self.index == 0 else 128
                ref = ref.at[pl.ds(way * half, half)]
            self.copies[way, edge] = remote(
                ref, ref, dens_send.at[self.index, way, edge], dens_recv.at[self.index, way, edge],
                device("x", step * (to - at)))

    from_sibling = []

    def share(place):
        group = wrap(x + RELATIVE[place])
        ref = vg.at[group, core]
        from_sibling.append(remote(ref, ref, sib_send.at[1, place], sib_recv.at[1, place], sibling))
        from_sibling.append(remote(
            og.at[group, pl.ds(4 - 4 * core, 4)], og_other.at[group],
            sib_send.at[0, place], sib_recv.at[0, place], sibling))

    first = []
    for s in (4, 3, -3, 2, -2, 1, -1):
        slot = s % N
        first.append(remote(og.at[x, y], og.at[x, y], first_send.at[0, slot], first_recv.at[0, slot], device("y", s)))
        first.append(remote(vs.at[z], vs.at[z], first_send.at[1, slot], first_recv.at[1, slot], device("z", s)))
    phase1 = []
    for p in range(3):
        phase1 += [Gather(2 * p, "z", xa, p), Gather(2 * p + 1, "y", xb, p)]
    dens = [Density(0), Density(1)]
    for g in phase1:
        g.advance(0)

    for copy in first:
        copy.wait_recv()
    vg[x, core] = vs[...].reshape(128, 256).T
    for d in dens:
        d.advance(0)
    share(0)
    for g in phase1:
        g.advance(1)
    for d in dens:
        d.advance(1)
    share(1)
    share(2)
    for g in phase1:
        g.advance(2)
    for d in dens:
        d.advance(2)
    share(3)
    share(4)
    for d in dens:
        d.finish()
    for place in (5, 6, 7):
        share(place)
    for copy in from_sibling:
        copy.wait_recv()
    for g in phase1:
        g.finish()

    def occ_rows(group):
        own = og[group, pl.ds(4 * core, 4)].reshape(128, 128)
        return jnp.concatenate([own, og_other[group].reshape(128, 128)], axis=1)

    def times_occ(buf, p):
        total = jnp.zeros((256, 256), jnp.float32)
        for place in range(0, N, 2):
            left = jnp.concatenate([buf[p, place], buf[p, place + 1]], axis=1)
            right = jnp.concatenate([occ_rows(wrap(z + RELATIVE[place + i])) for i in range(2)], axis=0)
            total += jnp.dot(left, right, preferred_element_type=jnp.float32)
        return total

    def virt_times(buf, p):
        total = jnp.zeros((256, 128), jnp.float32)
        for place in range(N):
            group = wrap(y + RELATIVE[place])
            left = jnp.concatenate([vg[group, 0], vg[group, 1]], axis=1)
            right = jnp.concatenate(
                [buf[p, place, :, 0].reshape(128, 128), buf[p, place, :, 1].reshape(128, 128)], axis=0)
            total += jnp.dot(left, right, preferred_element_type=jnp.float32)
        return total.astype(jnp.bfloat16)

    def hand_over(buf, p, index):
        total = times_occ(buf, p)
        mine[index] = total[:, :128]
        give[index] = total[:, 128:]
        return remote(give.at[index], got.at[index], part_send.at[index], part_recv.at[index], sibling)

    phase2, parts = [], []
    for p in range(3):
        phase2 += [Gather(6 + 2 * p, "z", gb, p), Gather(7 + 2 * p, "y", ha, p)]
    for p in range(3):
        parts.append(hand_over(xa, p, p))
        gb[p, 0] = virt_times(xb, p)
        phase2[2 * p].advance(0)
        parts[p].wait_recv()
        ha[p, 0] = (mine[p] + got[p]).astype(jnp.bfloat16).reshape(8, 2, 16, 128)
        phase2[2 * p + 1].advance(0)
    for g in phase2:
        g.advance(1)
    for g in phase2:
        g.advance(2)
    stores = []

    def put(p, value):
        outs[p] = value
        stores.append(pltpu.make_async_copy(outs.at[p], out_hbm.at[p], store_sem.at[p]))
        stores[-1].start()

    for p in range(3):
        phase2[2 * p].finish()
        parts.append(hand_over(gb, p, 3 + p))
        phase2[2 * p + 1].finish()
        put(p, virt_times(ha, p))
        parts[3 + p].wait_recv()
        put(3 + p, (mine[3 + p] + got[3 + p]).astype(jnp.bfloat16))
    for flight in started:
        flight.copy.wait_send()
    for store in stores:
        store.wait()


def on_device(three_centre, occ_density, virt_density, pair_mask, occ_mask, virt_mask, block_sizes):
    bf16 = jnp.bfloat16
    any_space = pl.BlockSpec(memory_space=pl.ANY)
    dma = pltpu.SemaphoreType.DMA
    edges = len(EDGES)
    out = pl.pallas_call(
        kernel,
        out_shape=jax.ShapeDtypeStruct((6, 256, 128), bf16),
        in_specs=[any_space] * 7,
        out_specs=any_space,
        scratch_shapes=[
            pltpu.SMEM((16, 16), jnp.int32),
            pltpu.SMEM((16, 16), jnp.int32),
            pltpu.SMEM((16, 16), jnp.int32),
            pltpu.SMEM((16,), jnp.int32),
            pltpu.VMEM((6, 256, 128), bf16),
            pltpu.VMEM((32, 128), bf16),
            pltpu.VMEM((16, 256), bf16),
            pltpu.VMEM((3, N, 256, 128), bf16),
            pltpu.VMEM((3, N, 8, 2, 16, 128), bf16),
            pltpu.VMEM((3, N, 8, 2, 16, 128), bf16),
            pltpu.VMEM((3, N, 256, 128), bf16),
            pltpu.VMEM((N, 8, 32, 128), bf16),
            pltpu.VMEM((N, 4, 32, 128), bf16),
            pltpu.VMEM((N, 16, 256), bf16),
            pltpu.VMEM((N, 2, 256, 128), bf16),
            pltpu.VMEM((6, 256, 128), jnp.float32),
            pltpu.VMEM((6, 256, 128), jnp.float32),
            pltpu.VMEM((6, 256, 128), jnp.float32),
            pltpu.VMEM((6, 256, 128), bf16),
            dma((12,)),
            dma((6,)),
            dma((2, N)),
            dma((2, N)),
            dma((2, 2, edges)),
            dma((2, 2, edges)),
            dma((12, 2, edges)),
            dma((12, 2, edges)),
            dma((6,)),
            dma((6,)),
            dma((2, N)),
            dma((2, N)),
        ],
        compiler_params=pltpu.CompilerParams(
            collective_id=0, has_side_effects=True, vmem_limit_bytes=60 << 20
        ),
        cost_estimate=pl.CostEstimate(flops=1610612736, bytes_accessed=1 << 20, transcendentals=0),
        name="transform",
    )(
        jnp.transpose(three_centre, (1, 0, 2)), occ_density.T, virt_density.T,
        pair_mask, occ_mask, virt_mask, block_sizes,
    )
    return jnp.transpose(out, (1, 0, 2))


def solution(mesh):
    placed = (
        P("layer", "row", "col"),
        P("col", ("row", "layer")),
        P("layer", ("row", "col")),
        P(),
        P(),
        P(),
        P(),
    )
    return jax.shard_map(
        on_device, mesh=mesh, in_specs=placed, out_specs=P("layer", "row", "col"), check_vma=False
    )
```

```python
import functools

import jax
import jax.numpy as jnp
from jax import lax
from jax.experimental import pallas as pl
from jax.experimental.pallas import tpu as pltpu
from jax.sharding import PartitionSpec as P

MESH = pl.DeviceIdType.MESH
BLOCK = 128
N = 8
RELATIVE = (0, -1, 1, -2, 2, -3, 3, 4)
PLACE = {0: 0, -1: 1, 1: 2, -2: 3, 2: 4, -3: 5, 3: 6, 4: 7, -4: 7}
TREE = (((0, 1),), ((1, 2),), ((2, 3), (2, 4)))
ARRIVALS = {(1, 0): 0, (1, 1): 1, (2, 0): 2, (2, 1): 3, (3, 0): 4, (3, 1): 4, (4, 0): 4, (4, 1): 4}
LAST = 4

def kernel(
    x_hbm, occ_hbm, virt_hbm, pair_hbm, occ_mask_hbm, virt_mask_hbm, sizes_hbm,
    out_hbm,
    pair_mask, occ_mask, virt_mask, sizes,
    x_raw, occ_raw, virt_raw, xa, xb, ha, gb, og, og_other, vs, vg, mine, give, got, held, outs,
    load_sem, store_sem, first_send, first_recv, dens_send, dens_recv,
    ring_send, ring_recv, part_send, part_recv, sib_send, sib_recv,
):
    x, col, y = lax.axis_index("row"), lax.axis_index("col"), lax.axis_index("layer")
    z, core = col // 2, lax.rem(col, 2)

    def wrap(i):
        return lax.rem(i + 2 * N, N)

    def device(axis, step):
        if axis == "x":
            return (wrap(x + step), col, y)
        if axis == "y":
            return (x, col, wrap(y + step))
        return (x, wrap(z + step) * 2 + core, y)

    sibling = (x, z * 2 + 1 - core, y)

    pairs = (
        (sizes_hbm, sizes), (occ_mask_hbm, occ_mask), (virt_mask_hbm, virt_mask), (pair_hbm, pair_mask),
        (occ_hbm, occ_raw), (virt_hbm, virt_raw), (x_hbm, x_raw),
    )
    loads = [pltpu.make_async_copy(src, dst, load_sem.at[i]) for i, (src, dst) in enumerate(pairs)]
    for load in loads:
        load.start()
    barrier = pltpu.get_barrier_semaphore()
    partners = [sibling]
    partners += [device("y", s) for s in range(1, N)] + [device("z", s) for s in range(1, N)]
    partners += [device("x", s) for s in (1, -1, 2, -2)]
    for partner in partners:
        pl.semaphore_signal(barrier, inc=1, device_id=partner, device_id_type=MESH)

    for load in loads[:5]:
        load.wait()
    n_block = 2 * x + y // 4
    n_living = (lax.rem(y, 4) * 32 + lax.broadcasted_iota(jnp.int32, (32, 128), 0)) < sizes[n_block]
    k_living = lax.broadcasted_iota(jnp.int32, (32, 128), 1) < sizes[col]
    o_keep = n_living & k_living & (occ_mask[n_block, col] > 0)
    og[x, y] = jnp.where(o_keep, occ_raw[...].astype(jnp.float32), 0.0).astype(jnp.bfloat16)
    loads[5].wait()
    m_block = 2 * x + col // 8
    m_living = (lax.rem(col, 8) * 16 + lax.broadcasted_iota(jnp.int32, (16, 128), 0)) < sizes[m_block]
    lane = lax.broadcasted_iota(jnp.int32, (16, 128), 1)
    for half in range(2):
        a_block = 2 * y + half
        v_keep = m_living & (lane < sizes[a_block]) & (virt_mask[a_block, m_block] > 0)
        part = virt_raw[:, half * 128 : half * 128 + 128].astype(jnp.float32)
        vs[z, :, half * 128 : half * 128 + 128] = jnp.where(v_keep, part, 0.0).astype(jnp.bfloat16)
    pl.semaphore_wait(barrier, len(partners))

    def remote(src, dst, send, recv, to):
        copy = pltpu.make_async_remote_copy(
            src_ref=src, dst_ref=dst, send_sem=send, recv_sem=recv, device_id=to, device_id_type=MESH)
        copy.start()
        return copy

    def wait_bytes(ref, sem):
        pltpu.make_async_copy(ref, ref, sem).wait()

    def window(buf, p, place, half):
        ref = buf.at[p, place]
        if half is None:
            return ref
        return ref.at[pl.ds(half * 128, 128)] if buf is xa or buf is gb else ref.at[pl.ds(half * 4, 4)]

    class Gather:
        def __init__(self, index, axis, buf, p):
            self.index, self.axis, self.buf, self.p, self.copies = index, axis, buf, p, {}

        def send(self, way, at, to):
            step = 1 - 2 * way
            half = way if to == 4 else None
            self.copies[way, to] = remote(
                window(self.buf, self.p, PLACE[-step * at], half),
                window(self.buf, self.p, PLACE[-step * to], half),
                ring_send.at[self.index // 3],
                ring_recv.at[self.index, ARRIVALS[to, way]],
                device(self.axis, step * (to - at)),
            )

        def advance(self, stage):
            for way in range(2):
                if stage > 0:
                    self.copies[way, stage].wait_recv()
                for at, to in TREE[stage]:
                    self.send(way, at, to)

        def finish(self):
            wait_bytes(self.buf.at[self.p, pl.ds(5, 3)], ring_recv.at[self.index, LAST])

    class Density(Gather):
        def __init__(self, index):
            self.index, self.copies = index, {}

        def send(self, way, at, to):
            step = 1 - 2 * way
            group = wrap(x - step * at)
            ref = og.at[group] if self.index == 0 else vg.at[group, core]
            if to == 4:
                half = 4 if self.index == 0 else 128
                ref = ref.at[pl.ds(way * half, half)]
            self.copies[way, to] = remote(
                ref, ref, dens_send.at[self.index], dens_recv.at[self.index, ARRIVALS[to, way]],
                device("x", step * (to - at)))

        def finish(self):
            ref = og.at[pl.ds(0, 3)] if self.index == 0 else vg.at[pl.ds(0, 3), 0]
            wait_bytes(ref, dens_recv.at[self.index, LAST])

    def share(place):
        group = wrap(x + RELATIVE[place])
        ref, late = vg.at[group, core], place // 4
        remote(ref, ref, sib_send.at[1], sib_recv.at[1, late], sibling)
        remote(og.at[group, pl.ds(4 - 4 * core, 4)], og_other.at[group], sib_send.at[0], sib_recv.at[0, late], sibling)

    def shared_arrived(late):
        wait_bytes(og_other.at[pl.ds(0, 4)], sib_recv.at[0, late])
        wait_bytes(vg.at[pl.ds(0, 4), 0], sib_recv.at[1, late])

    def first_step():
        for s in (4, 3, -3, 2, -2, 1, -1):
            remote(og.at[x, y], og.at[x, y], first_send.at[0], first_recv.at[0], device("y", s))
            remote(vs.at[z], vs.at[z], first_send.at[1], first_recv.at[1], device("z", s))

    dens = [Density(0), Density(1)]

    def groups_ready():
        wait_bytes(og.at[x, pl.ds(0, 7)], first_recv.at[0])
        dens[0].advance(0)
        wait_bytes(vs.at[pl.ds(0, 7)], first_recv.at[1])
        vg[x, core] = vs[...].reshape(128, 256).T
        dens[1].advance(0)
        share(0)

    def groups_pass(stage):
        for d in dens:
            d.advance(stage)
        share(2 * stage - 1)
        share(2 * stage)

    def groups_done():
        for d in dens:
            d.finish()
        for place in (5, 6, 7):
            share(place)

    def occ_rows(group):
        own = og[group, pl.ds(4 * core, 4)].reshape(128, 128)
        return jnp.concatenate([own, og_other[group].reshape(128, 128)], axis=1)

    def place_of(group, here):
        apart = wrap(group - here)
        return jnp.minimum(2 * apart, 15 - 2 * apart)

    def times_occ(buf, p, pairs):
        left = jnp.concatenate([buf[p, place] for place, _ in pairs], axis=1)
        right = jnp.concatenate([occ_rows(group) for _, group in pairs], axis=0)
        return jnp.dot(left, right, preferred_element_type=jnp.float32)

    def virt_times(buf, p, pairs):
        left = jnp.concatenate([vg[group, half] for _, group in pairs for half in range(2)], axis=1)
        right = jnp.concatenate(
            [buf[p, place, :, half].reshape(128, 128) for place, _ in pairs for half in range(2)], axis=0)
        return jnp.dot(left, right, preferred_element_type=jnp.float32)

    def occ_early(buf, p, index, pairs):
        total = times_occ(buf, p, pairs)
        mine[index] = total[:, :128]
        give[index] = total[:, 128:]

    def occ_late(buf, p, index, pairs):
        total = times_occ(buf, p, pairs)
        give[index] += total[:, 128:]
        parts[index] = remote(give.at[index], got.at[index], part_send.at[0], part_recv.at[index], sibling)
        mine[index] += total[:, :128]

    def occ_total(index):
        parts[index].wait_recv()
        return (mine[index] + got[index]).astype(jnp.bfloat16)

    def virt_early(buf, p, index, pairs):
        held[index] = virt_times(buf, p, pairs)

    def virt_late(buf, p, index, pairs):
        return (held[index] + virt_times(buf, p, pairs)).astype(jnp.bfloat16)

    parts = {}
    by_group = [wrap(x + RELATIVE[i]) for i in range(N)]
    occ1 = [(place_of(group, z), group) for group in by_group]
    virt1 = [(place_of(group, y), group) for group in by_group]
    occ2 = [(i, wrap(z + RELATIVE[i])) for i in range(N)]
    virt2 = [(i, wrap(y + RELATIVE[i])) for i in range(N)]
    phase1 = [(Gather(p, "z", xa, p), Gather(3 + p, "y", xb, p)) for p in range(3)]
    phase2 = [(Gather(6 + p, "z", gb, p), Gather(9 + p, "y", ha, p)) for p in range(3)]

    def both(p, stage):
        for g in phase1[p]:
            g.advance(stage)

    def shards_done():
        for pair in phase1:
            for g in pair:
                g.finish()

    def early():
        for p in range(3):
            occ_early(xa, p, p, occ1[:4])
            virt_early(xb, p, p, virt1[:4])

    first_step()
    loads[6].wait()
    keep = [jnp.where(pair_mask[2 * y + half, col] > 0, 1.0, 0.0).astype(jnp.bfloat16) for half in range(2)]
    for p in range(3):
        for half in range(2):
            rows = pl.ds(half * 128, 128)
            xa[p, 0, rows] = x_raw[p, rows] * keep[half]
            xb[p, 0, pl.ds(half * 4, 4)] = (x_raw[3 + p, rows] * keep[half]).reshape(4, 2, 16, 128)
        both(p, 0)
    tasks = [(4.2, groups_ready)]
    for p in range(3):
        for stage in range(1, len(TREE)):
            tasks.append((3.6 + 0.8 * p + 3.2 * (stage - 1), functools.partial(both, p, stage)))
    for stage in range(1, len(TREE)):
        tasks.append((7.5 + 3.3 * (stage - 1), functools.partial(groups_pass, stage)))
    for _, task in sorted(tasks, key=lambda entry: entry[0]):
        task()
    shards_done()
    shared_arrived(0)
    early()
    groups_done()
    shared_arrived(1)

    def begin_b(p):
        gb[p, 0] = virt_late(xb, p, p, virt1[4:])
        phase2[p][0].advance(0)

    def begin_a(p):
        ha[p, 0] = occ_total(p).reshape(8, 2, 16, 128)
        phase2[p][1].advance(0)

    for p in range(3):
        occ_late(xa, p, p, occ1[4:])
    for p in range(3):
        begin_b(p)
        begin_a(p)
    for stage in range(1, len(TREE)):
        for p in range(3):
            for g in phase2[p]:
                g.advance(stage)
    for p in range(3):
        occ_early(gb, p, 3 + p, occ2[:4])
        virt_early(ha, p, 3 + p, virt2[:4])
    def put(p, value):
        outs[p] = value
        pltpu.make_async_copy(outs.at[p], out_hbm.at[p], store_sem.at[0]).start()

    for p in range(3):
        phase2[p][0].finish()
        occ_late(gb, p, 3 + p, occ2[4:])
        phase2[p][1].finish()
        put(p, virt_late(ha, p, 3 + p, virt2[4:]))
        put(3 + p, occ_total(3 + p))
    for i, buf in enumerate((xa, xb, gb, ha)):
        wait_bytes(buf.at[:, pl.ds(0, 7)], ring_send.at[i])
    wait_bytes(og.at[pl.ds(0, 7)], dens_send.at[0])
    wait_bytes(vg.at[pl.ds(0, 7), 0], dens_send.at[1])
    wait_bytes(og.at[0, pl.ds(0, 7)], first_send.at[0])
    wait_bytes(vs.at[pl.ds(0, 7)], first_send.at[1])
    wait_bytes(og_other, sib_send.at[0])
    wait_bytes(vg.at[:, 0], sib_send.at[1])
    wait_bytes(give, part_send.at[0])
    wait_bytes(outs, store_sem.at[0])


def on_device(three_centre, occ_density, virt_density, pair_mask, occ_mask, virt_mask, block_sizes):
    bf16 = jnp.bfloat16
    any_space = pl.BlockSpec(memory_space=pl.ANY)
    dma = pltpu.SemaphoreType.DMA
    out = pl.pallas_call(
        kernel,
        out_shape=jax.ShapeDtypeStruct((6, 256, 128), bf16),
        in_specs=[any_space] * 7,
        out_specs=any_space,
        scratch_shapes=[
            pltpu.SMEM((16, 16), jnp.int32),
            pltpu.SMEM((16, 16), jnp.int32),
            pltpu.SMEM((16, 16), jnp.int32),
            pltpu.SMEM((16,), jnp.int32),
            pltpu.VMEM((6, 256, 128), bf16),
            pltpu.VMEM((32, 128), bf16),
            pltpu.VMEM((16, 256), bf16),
            pltpu.VMEM((3, N, 256, 128), bf16),
            pltpu.VMEM((3, N, 8, 2, 16, 128), bf16),
            pltpu.VMEM((3, N, 8, 2, 16, 128), bf16),
            pltpu.VMEM((3, N, 256, 128), bf16),
            pltpu.VMEM((N, 8, 32, 128), bf16),
            pltpu.VMEM((N, 4, 32, 128), bf16),
            pltpu.VMEM((N, 16, 256), bf16),
            pltpu.VMEM((N, 2, 256, 128), bf16),
            pltpu.VMEM((6, 256, 128), jnp.float32),
            pltpu.VMEM((6, 256, 128), jnp.float32),
            pltpu.VMEM((6, 256, 128), jnp.float32),
            pltpu.VMEM((6, 256, 128), jnp.float32),
            pltpu.VMEM((6, 256, 128), bf16),
            dma((7,)),
            dma((1,)),
            dma((2,)),
            dma((2,)),
            dma((2,)),
            dma((2, 5)),
            dma((4,)),
            dma((12, 5)),
            dma((1,)),
            dma((6,)),
            dma((2,)),
            dma((2, 2)),
        ],
        compiler_params=pltpu.CompilerParams(
            collective_id=0, has_side_effects=True, vmem_limit_bytes=60 << 20
        ),
        cost_estimate=pl.CostEstimate(flops=1610612736, bytes_accessed=1 << 20, transcendentals=0),
        name="transform",
    )(
        jnp.transpose(three_centre, (1, 0, 2)), occ_density.T, virt_density.T,
        pair_mask, occ_mask, virt_mask, block_sizes,
    )
    return jnp.transpose(out, (1, 0, 2))


def solution(mesh):
    placed = (
        P("layer", "row", "col"),
        P("col", ("row", "layer")),
        P("layer", ("row", "col")),
        P(),
        P(),
        P(),
        P(),
    )
    return jax.shard_map(
        on_device, mesh=mesh, in_specs=placed, out_specs=P("layer", "row", "col"), check_vma=False
    )
```

```python
import functools

import jax
import jax.numpy as jnp
from jax import lax
from jax.experimental import pallas as pl
from jax.experimental.pallas import tpu as pltpu
from jax.sharding import PartitionSpec as P

MESH = pl.DeviceIdType.MESH
BLOCK = 128
N = 8
RELATIVE = (0, -1, 1, -2, 2, -3, 3, 4)
PLACE = {0: 0, -1: 1, 1: 2, -2: 3, 2: 4, -3: 5, 3: 6, 4: 7, -4: 7}
TREE = (((0, 1),), ((1, 2),), ((2, 4), (2, 3)))
ARRIVALS = {(1, 0): 0, (1, 1): 1, (2, 0): 2, (2, 1): 3, (3, 0): 4, (3, 1): 4, (4, 0): 4, (4, 1): 4}
LAST = 4

def kernel(
    x_hbm, occ_hbm, virt_hbm, pair_hbm, occ_mask_hbm, virt_mask_hbm, sizes_hbm,
    out_hbm,
    pair_mask, occ_mask, virt_mask, sizes,
    x_raw, occ_raw, virt_raw, xa, xb, ha, gb, og, og_other, vs, vg, mine, give, got, held, outs,
    load_sem, store_sem, first_send, first_recv, dens_send, dens_recv,
    ring_send, ring_recv, part_send, part_recv, sib_send, sib_recv,
):
    x, col, y = lax.axis_index("row"), lax.axis_index("col"), lax.axis_index("layer")
    z, core = col // 2, lax.rem(col, 2)

    def wrap(i):
        return lax.rem(i + 2 * N, N)

    def device(axis, step):
        if axis == "x":
            return (wrap(x + step), col, y)
        if axis == "y":
            return (x, col, wrap(y + step))
        return (x, wrap(z + step) * 2 + core, y)

    sibling = (x, z * 2 + 1 - core, y)

    pairs = (
        (sizes_hbm, sizes), (occ_mask_hbm, occ_mask), (virt_mask_hbm, virt_mask), (pair_hbm, pair_mask),
        (occ_hbm, occ_raw), (virt_hbm, virt_raw), (x_hbm, x_raw),
    )
    loads = [pltpu.make_async_copy(src, dst, load_sem.at[i]) for i, (src, dst) in enumerate(pairs)]
    for load in loads:
        load.start()
    barrier = pltpu.get_barrier_semaphore()
    partners = [sibling]
    partners += [device("y", s) for s in range(1, N)] + [device("z", s) for s in range(1, N)]
    partners += [device("x", s) for s in (1, -1, 2, -2)]
    for partner in partners:
        pl.semaphore_signal(barrier, inc=1, device_id=partner, device_id_type=MESH)

    for load in loads[:5]:
        load.wait()
    n_block = 2 * x + y // 4
    n_living = (lax.rem(y, 4) * 32 + lax.broadcasted_iota(jnp.int32, (32, 128), 0)) < sizes[n_block]
    k_living = lax.broadcasted_iota(jnp.int32, (32, 128), 1) < sizes[col]
    o_keep = n_living & k_living & (occ_mask[n_block, col] > 0)
    og[x, y] = jnp.where(o_keep, occ_raw[...].astype(jnp.float32), 0.0).astype(jnp.bfloat16)
    loads[5].wait()
    m_block = 2 * x + col // 8
    m_living = (lax.rem(col, 8) * 16 + lax.broadcasted_iota(jnp.int32, (16, 128), 0)) < sizes[m_block]
    lane = lax.broadcasted_iota(jnp.int32, (16, 128), 1)
    for half in range(2):
        a_block = 2 * y + half
        v_keep = m_living & (lane < sizes[a_block]) & (virt_mask[a_block, m_block] > 0)
        part = virt_raw[:, half * 128 : half * 128 + 128].astype(jnp.float32)
        vs[z, :, half * 128 : half * 128 + 128] = jnp.where(v_keep, part, 0.0).astype(jnp.bfloat16)
    pl.semaphore_wait(barrier, len(partners))

    def remote(src, dst, send, recv, to):
        copy = pltpu.make_async_remote_copy(
            src_ref=src, dst_ref=dst, send_sem=send, recv_sem=recv, device_id=to, device_id_type=MESH)
        copy.start()
        return copy

    def wait_bytes(ref, sem):
        pltpu.make_async_copy(ref, ref, sem).wait()

    def window(buf, p, place, half):
        ref = buf.at[p, place]
        if half is None:
            return ref
        return ref.at[pl.ds(half * 128, 128)] if buf is xa or buf is gb else ref.at[pl.ds(half * 4, 4)]

    class Gather:
        def __init__(self, index, axis, buf, p):
            self.index, self.axis, self.buf, self.p, self.copies = index, axis, buf, p, {}

        def send(self, way, at, to):
            step = 1 - 2 * way
            half = way if to == 4 else None
            self.copies[way, to] = remote(
                window(self.buf, self.p, PLACE[-step * at], half),
                window(self.buf, self.p, PLACE[-step * to], half),
                ring_send.at[self.index // 3],
                ring_recv.at[self.index, ARRIVALS[to, way]],
                device(self.axis, step * (to - at)),
            )

        def advance(self, stage):
            for way in range(2):
                if stage > 0:
                    self.copies[way, stage].wait_recv()
                for at, to in TREE[stage]:
                    self.send(way, at, to)

        def finish(self):
            wait_bytes(self.buf.at[self.p, pl.ds(5, 3)], ring_recv.at[self.index, LAST])

    class Density(Gather):
        def __init__(self, index):
            self.index, self.copies = index, {}

        def send(self, way, at, to):
            step = 1 - 2 * way
            group = wrap(x - step * at)
            ref = og.at[group] if self.index == 0 else vg.at[group, core]
            if to == 4:
                half = 4 if self.index == 0 else 128
                ref = ref.at[pl.ds(way * half, half)]
            self.copies[way, to] = remote(
                ref, ref, dens_send.at[self.index], dens_recv.at[self.index, 2 * to - 2 + way if to < 4 else 6],
                device("x", step * (to - at)))

        def finish(self):
            wait_bytes(og.at[0] if self.index == 0 else vg.at[0, 0], dens_recv.at[self.index, 6])

    def share(place):
        group = wrap(x + RELATIVE[place])
        ref, late = vg.at[group, core], place // 4
        remote(ref, ref, sib_send.at[1], sib_recv.at[1, late], sibling)
        remote(og.at[group, pl.ds(4 - 4 * core, 4)], og_other.at[group], sib_send.at[0], sib_recv.at[0, late], sibling)

    def shared_arrived(late):
        wait_bytes(og_other.at[pl.ds(0, 4)], sib_recv.at[0, late])
        wait_bytes(vg.at[pl.ds(0, 4), 0], sib_recv.at[1, late])

    def first_step():
        for s in (4, 3, -3, 2, -2, 1, -1):
            remote(og.at[x, y], og.at[x, y], first_send.at[0], first_recv.at[0], device("y", s))
            remote(vs.at[z], vs.at[z], first_send.at[1], first_recv.at[1], device("z", s))

    dens = [Density(0), Density(1)]

    def groups_ready():
        wait_bytes(og.at[x, pl.ds(0, 7)], first_recv.at[0])
        dens[0].advance(0)
        wait_bytes(vs.at[pl.ds(0, 7)], first_recv.at[1])
        vg[x, core] = vs[...].reshape(128, 256).T
        dens[1].advance(0)
        share(0)

    def groups_pass(stage):
        for d in dens:
            d.advance(stage)
        share(2 * stage - 1)
        share(2 * stage)

    def groups_done():
        for way in range(2):
            for d in dens:
                d.copies[way, 3].wait_recv()
            share(5 + way)
        for d in dens:
            d.finish()
        share(7)

    def occ_rows(group):
        own = og[group, pl.ds(4 * core, 4)].reshape(128, 128)
        return jnp.concatenate([own, og_other[group].reshape(128, 128)], axis=1)

    def place_of(group, here):
        apart = wrap(group - here)
        return jnp.minimum(2 * apart, 15 - 2 * apart)

    def times_occ(buf, p, pairs):
        left = jnp.concatenate([buf[p, place] for place, _ in pairs], axis=1)
        right = jnp.concatenate([occ_rows(group) for _, group in pairs], axis=0)
        return jnp.dot(left, right, preferred_element_type=jnp.float32)

    def virt_times(buf, p, pairs):
        left = jnp.concatenate([vg[group, half] for _, group in pairs for half in range(2)], axis=1)
        right = jnp.concatenate(
            [buf[p, place, :, half].reshape(128, 128) for place, _ in pairs for half in range(2)], axis=0)
        return jnp.dot(left, right, preferred_element_type=jnp.float32)

    def occ_early(buf, p, index, pairs):
        total = times_occ(buf, p, pairs)
        mine[index] = total[:, :128]
        give[index] = total[:, 128:]

    def occ_late(buf, p, index, pairs):
        total = times_occ(buf, p, pairs)
        give[index] += total[:, 128:]
        parts[index] = remote(give.at[index], got.at[index], part_send.at[0], part_recv.at[index], sibling)
        mine[index] += total[:, :128]

    def occ_total(index):
        parts[index].wait_recv()
        return (mine[index] + got[index]).astype(jnp.bfloat16)

    def virt_early(buf, p, index, pairs):
        held[index] = virt_times(buf, p, pairs)

    def virt_late(buf, p, index, pairs):
        return (held[index] + virt_times(buf, p, pairs)).astype(jnp.bfloat16)

    parts = {}
    by_group = [wrap(x + RELATIVE[i]) for i in range(N)]
    occ1 = [(place_of(group, z), group) for group in by_group]
    virt1 = [(place_of(group, y), group) for group in by_group]
    occ2 = [(i, wrap(z + RELATIVE[i])) for i in range(N)]
    virt2 = [(i, wrap(y + RELATIVE[i])) for i in range(N)]
    phase1 = [(Gather(p, "z", xa, p), Gather(3 + p, "y", xb, p)) for p in range(3)]
    phase2 = [(Gather(6 + p, "z", gb, p), Gather(9 + p, "y", ha, p)) for p in range(3)]

    def both(p, stage):
        for g in phase1[p]:
            g.advance(stage)

    def shards_done():
        for pair in phase1:
            for g in pair:
                g.finish()

    def early():
        for p in range(3):
            occ_early(xa, p, p, occ1[:4])
            virt_early(xb, p, p, virt1[:4])

    first_step()
    loads[6].wait()
    keep = [jnp.where(pair_mask[2 * y + half, col] > 0, 1.0, 0.0).astype(jnp.bfloat16) for half in range(2)]
    for p in range(3):
        for half in range(2):
            rows = pl.ds(half * 128, 128)
            xa[p, 0, rows] = x_raw[p, rows] * keep[half]
            xb[p, 0, pl.ds(half * 4, 4)] = (x_raw[3 + p, rows] * keep[half]).reshape(4, 2, 16, 128)
        both(p, 0)
    tasks = [(4.2, groups_ready)]
    for p in range(3):
        for stage in range(1, len(TREE)):
            tasks.append((3.6 + 0.8 * p + 3.2 * (stage - 1), functools.partial(both, p, stage)))
    for stage in range(1, len(TREE)):
        tasks.append((7.5 + 3.3 * (stage - 1), functools.partial(groups_pass, stage)))
    for _, task in sorted(tasks, key=lambda entry: entry[0]):
        task()
    shards_done()
    shared_arrived(0)
    early()
    groups_done()
    shared_arrived(1)

    def begin_b(p):
        gb[p, 0] = virt_late(xb, p, p, virt1[4:])
        phase2[p][0].advance(0)

    def begin_a(p):
        ha[p, 0] = occ_total(p).reshape(8, 2, 16, 128)
        phase2[p][1].advance(0)

    for p in range(3):
        occ_late(xa, p, p, occ1[4:])
    for p in range(3):
        begin_b(p)
        begin_a(p)
    for stage in range(1, len(TREE)):
        for p in range(3):
            for g in phase2[p]:
                g.advance(stage)
    for p in range(3):
        occ_early(gb, p, 3 + p, occ2[:4])
        virt_early(ha, p, 3 + p, virt2[:4])
    def put(p, value):
        outs[p] = value
        pltpu.make_async_copy(outs.at[p], out_hbm.at[p], store_sem.at[0]).start()

    for p in range(3):
        phase2[p][0].finish()
        occ_late(gb, p, 3 + p, occ2[4:])
        phase2[p][1].finish()
        put(p, virt_late(ha, p, 3 + p, virt2[4:]))
        put(3 + p, occ_total(3 + p))
    for i, buf in enumerate((xa, xb, gb, ha)):
        wait_bytes(buf.at[:, pl.ds(0, 7)], ring_send.at[i])
    wait_bytes(og.at[pl.ds(0, 7)], dens_send.at[0])
    wait_bytes(vg.at[pl.ds(0, 7), 0], dens_send.at[1])
    wait_bytes(og.at[0, pl.ds(0, 7)], first_send.at[0])
    wait_bytes(vs.at[pl.ds(0, 7)], first_send.at[1])
    wait_bytes(og_other, sib_send.at[0])
    wait_bytes(vg.at[:, 0], sib_send.at[1])
    wait_bytes(give, part_send.at[0])
    wait_bytes(outs, store_sem.at[0])


def on_device(three_centre, occ_density, virt_density, pair_mask, occ_mask, virt_mask, block_sizes):
    bf16 = jnp.bfloat16
    any_space = pl.BlockSpec(memory_space=pl.ANY)
    dma = pltpu.SemaphoreType.DMA
    out = pl.pallas_call(
        kernel,
        out_shape=jax.ShapeDtypeStruct((6, 256, 128), bf16),
        in_specs=[any_space] * 7,
        out_specs=any_space,
        scratch_shapes=[
            pltpu.SMEM((16, 16), jnp.int32),
            pltpu.SMEM((16, 16), jnp.int32),
            pltpu.SMEM((16, 16), jnp.int32),
            pltpu.SMEM((16,), jnp.int32),
            pltpu.VMEM((6, 256, 128), bf16),
            pltpu.VMEM((32, 128), bf16),
            pltpu.VMEM((16, 256), bf16),
            pltpu.VMEM((3, N, 256, 128), bf16),
            pltpu.VMEM((3, N, 8, 2, 16, 128), bf16),
            pltpu.VMEM((3, N, 8, 2, 16, 128), bf16),
            pltpu.VMEM((3, N, 256, 128), bf16),
            pltpu.VMEM((N, 8, 32, 128), bf16),
            pltpu.VMEM((N, 4, 32, 128), bf16),
            pltpu.VMEM((N, 16, 256), bf16),
            pltpu.VMEM((N, 2, 256, 128), bf16),
            pltpu.VMEM((6, 256, 128), jnp.float32),
            pltpu.VMEM((6, 256, 128), jnp.float32),
            pltpu.VMEM((6, 256, 128), jnp.float32),
            pltpu.VMEM((6, 256, 128), jnp.float32),
            pltpu.VMEM((6, 256, 128), bf16),
            dma((7,)),
            dma((1,)),
            dma((2,)),
            dma((2,)),
            dma((2,)),
            dma((2, 7)),
            dma((4,)),
            dma((12, 5)),
            dma((1,)),
            dma((6,)),
            dma((2,)),
            dma((2, 2)),
        ],
        compiler_params=pltpu.CompilerParams(
            collective_id=0, has_side_effects=True, vmem_limit_bytes=60 << 20
        ),
        cost_estimate=pl.CostEstimate(flops=1610612736, bytes_accessed=1 << 20, transcendentals=0),
        name="transform",
    )(
        jnp.transpose(three_centre, (1, 0, 2)), occ_density.T, virt_density.T,
        pair_mask, occ_mask, virt_mask, block_sizes,
    )
    return jnp.transpose(out, (1, 0, 2))


def solution(mesh):
    placed = (
        P("layer", "row", "col"),
        P("col", ("row", "layer")),
        P("layer", ("row", "col")),
        P(),
        P(),
        P(),
        P(),
    )
    return jax.shard_map(
        on_device, mesh=mesh, in_specs=placed, out_specs=P("layer", "row", "col"), check_vma=False
    )
```
